32 devices in a mesh: groups: 2 (over y), gene: 8 (over z, x), cell: 2 (over core).
Axes of the slice: x: 2, y: 2, z: 4, core: 2. Of those that a mesh axis runs over, the one named last changes fastest.
Arguments:
- control: bfloat16 [512, 32768], P(('groups', 'cell'), 'gene'), parts along dimension 0, may hold values from -6 to 6
- perturbed: bfloat16 [512, 32768], P(('groups', 'cell'), 'gene'), parts along dimension 0, may hold values from -6 to 6
- pair_index: int32 [4, 128], P(('groups', 'cell')), parts along dimension 0, may hold values from 0 to 127, each once within a row
- noise_draws: bfloat16 [512, 2, 128], P(('groups', 'cell')), parts along dimension 0, may hold values from -6 to 6
- cell_mass: float32 [512], P(('groups', 'cell')), parts along dimension 0, may hold values from 0.25 to 4
- w_enc: bfloat16 [32768, 4096], P(('gene', 'cell')), may hold values from -0.03125 to 0.03125
- w_dec: bfloat16 [32768, 4096], P(('gene', 'cell')), may hold values from -0.09375 to 0.09375
- w_crit: bfloat16 [32768, 4096], P(('gene', 'cell')), may hold values from -0.03125 to 0.03125
- w_noise: bfloat16 [128, 4096], P(None, 'gene'), may hold values from -0.5 to 0.5
- readout: float32 [4096], P('gene'), may hold values from -0.09375 to 0.09375
Outputs:
- grad_enc: bfloat16 [65536, 4096], P(('groups', 'gene', 'cell')), parts along dimension 0
- grad_dec: bfloat16 [65536, 4096], P(('groups', 'gene', 'cell')), parts along dimension 0
The draws below stay inside these ranges and needn't reach their ends.
There are 2 independent parts, one for each index of `groups`. The reference program is written for one: setup_inputs(seed, part) draws one part's arguments, and reference() takes and returns one part's arrays. A program takes and returns all parts, laid end to end along the dimension named above; an argument that names none is the same for every part. Nothing has to cross between parts.
Inputs may be any that keep to these rules, and one draw needn't show every extreme that they name: Each row of pair_index is a permutation of 0 to 127.
All inputs are finite; a program needn't handle non-finite values.
Results may differ from the reference program's by a relative error of at most 0.0065.
Values may be sent and summed in bfloat16 or wider, within the bound.
A program may use at most 512 MiB of HBM per device.

```python
import math
import jax
import jax.numpy as jnp
from jax import lax

G = 32768
H = 4096
NZ = 128
DRAWS = 2
B_DEV = 128
CELLS = 256
N_CELL = 2


def levels(own_key, extent, pieces, low, high):
    level, own = 1.0, jax.random.fold_in(own_key, 6)
    for dim, blocks in pieces:
        draws = jnp.exp(jax.random.uniform(jax.random.fold_in(own, dim), (blocks,), jnp.float32, low / len(pieces), high / len(pieces)))
        level = level * jnp.repeat(draws, extent[dim] // blocks).reshape([-1 if axis == dim else 1 for axis in range(len(extent))])
    return level


def noise(own_key, shape, width, limit, cuts=(), held_as=jnp.bfloat16):
    drawn = jax.random.normal(own_key, shape, jnp.float32) * width
    if len(cuts) > 0:
        drawn = levels(own_key, shape, cuts, -0.22, 0.18) * drawn
    return jnp.clip(drawn, min=-limit, max=limit).astype(held_as)


def setup_inputs(seed: int = 0, part: int = 0) -> dict:
    key_list = jax.random.split(jax.random.key(seed), 11)
    part_keys = jax.random.split(jax.random.fold_in(key_list[10], part), 11)
    control = noise(part_keys[0], (CELLS, G), 1.0, 6.0, ((0, 2), (1, 8)))
    perturbed = noise(part_keys[1], (CELLS, G), 1.0, 6.0, ((0, 2), (1, 8)))
    pair_index = jax.vmap(lambda own: jax.random.permutation(own, B_DEV))(jax.random.split(part_keys[2], N_CELL)).reshape((N_CELL, B_DEV)).astype(jnp.int32)
    noise_draws = noise(part_keys[3], (CELLS, DRAWS, NZ), 1.0, 6.0, ((0, 2),))
    cell_mass = jnp.clip(jnp.exp(math.log(4.0) - 2.7725887 * jax.random.uniform(part_keys[4], (CELLS,), jnp.float32) ** levels(part_keys[4], (CELLS,), ((0, 2),), -0.2, 0.2)), 0.25, 4.0)
    w_enc = noise(key_list[5], (G, H), G ** -0.5, 0.03125, ((0, 16),))
    w_dec = noise(key_list[6], (G, H), H ** -0.5, 0.09375, ((0, 16),))
    w_crit = noise(key_list[7], (G, H), G ** -0.5, 0.03125, ((0, 16),))
    w_noise = noise(key_list[8], (NZ, H), NZ ** -0.5, 0.5, ((1, 8),))
    readout = noise(key_list[9], (H,), H ** -0.5, 0.09375, ((0, 8),), jnp.float32)
    return {"control": control, "perturbed": perturbed, "pair_index": pair_index, "noise_draws": noise_draws, "cell_mass": cell_mass, "w_enc": w_enc, "w_dec": w_dec, "w_crit": w_crit, "w_noise": w_noise, "readout": readout}


def silu_grad(inputs):
    sigmoid = jax.nn.sigmoid(inputs)
    return sigmoid * (1.0 + inputs * (1.0 - sigmoid))

def reference(control, perturbed, pair_index, noise_draws, cell_mass, w_enc, w_dec, w_crit, w_noise, readout):
    n_cells = control.shape[0]
    n_draws = noise_draws.shape[1]
    offsets = (jnp.arange(N_CELL, dtype=jnp.int32) * B_DEV)[:, None]
    chosen = (pair_index.astype(jnp.int32) + offsets).reshape(n_cells)
    target = perturbed[chosen].astype(jnp.float32)
    enc = jnp.dot(control, w_enc, preferred_element_type=jnp.float32)
    flat_noise = noise_draws.reshape(n_cells * n_draws, NZ)
    noise_shift = jnp.dot(flat_noise, w_noise, preferred_element_type=jnp.float32).reshape(n_cells, n_draws, H)
    latent = (jax.nn.silu(enc)[:, None, :] + noise_shift).astype(jnp.bfloat16).reshape(n_cells * n_draws, H)
    decoded = jnp.dot(latent, w_dec.T, preferred_element_type=jnp.float32).reshape(n_cells, n_draws, G)
    moved = (control.astype(jnp.float32)[:, None, :] + decoded).astype(jnp.bfloat16)
    flat_moved = moved.reshape(n_cells * n_draws, G)
    critic_pre = jnp.dot(flat_moved, w_crit, preferred_element_type=jnp.float32)
    weight = 8.0 / n_draws * jnp.repeat(cell_mass, n_draws)
    critic_grad = (-weight[:, None] * readout[None, :] * silu_grad(critic_pre)).astype(jnp.bfloat16)
    moved_f32 = moved.astype(jnp.float32)
    mean_moved = lax.optimization_barrier(jnp.sum(moved_f32, axis=1, keepdims=True)) / n_draws
    cost_grad = 8.0 / (n_draws * math.sqrt(G)) * cell_mass[:, None, None] * (0.5 * moved_f32 + 0.5 * mean_moved - target[:, None, :])
    critic_back = jnp.dot(critic_grad, w_crit.T, preferred_element_type=jnp.float32)
    moved_grad = (cost_grad.reshape(n_cells * n_draws, G) + critic_back).astype(jnp.bfloat16)
    grad_dec = jnp.dot(moved_grad.T, latent, preferred_element_type=jnp.float32).astype(jnp.bfloat16)
    latent_grad = jnp.dot(moved_grad, w_dec, preferred_element_type=jnp.float32).reshape(n_cells, n_draws, H)
    enc_grad = (silu_grad(enc) * lax.optimization_barrier(jnp.sum(latent_grad, axis=1))).astype(jnp.bfloat16)
    grad_enc = jnp.dot(control.T, enc_grad, preferred_element_type=jnp.float32).astype(jnp.bfloat16)
    return (grad_enc, grad_dec)
```

```python
import functools
import math

import jax
import jax.numpy as jnp
from jax import lax
from jax.experimental import pallas as pl
from jax.experimental.pallas import tpu as pltpu
from jax.sharding import PartitionSpec as P

G = 32768
MESH = pl.DeviceIdType.MESH
F32 = jnp.float32
BF16 = jnp.bfloat16


def silu_grad(inputs):
    sigmoid = 1.0 / (1.0 + jnp.exp(-inputs))
    return sigmoid * (1.0 + inputs * (1.0 - sigmoid))


def contract(former, latter, former_dim, latter_dim):
    return lax.dot_general(
        former,
        latter,
        (((former_dim,), (latter_dim,)), ((), ())),
        preferred_element_type=F32,
    )


def row_loop(n_rows, tile, body):
    def step(i, carry):
        body(pl.ds(pl.multiple_of(i * tile, tile), tile), pl.multiple_of(i * tile, tile))
        return carry

    lax.fori_loop(0, n_rows // tile, step, 0)


def exchange_kernel(kind, nz, nx, nch, *refs):
    if kind == "enc":
        p_ref, g_ref, e_ref = refs[:3]
        rest = refs[3:]
    elif kind == "crit":
        p_ref, weight_ref, readout_ref, g_ref = refs[:4]
        rest = refs[4:]
    else:
        p_ref, e_ref, g_ref = refs[:3]
        rest = refs[3:]
    (c_buf, s1_buf, x_buf, s2_buf, z_buf) = rest[:5]
    sems = rest[5:]
    cs_send, cs_recv, xs_send, xs_recv, zs_send, zs_recv = sems[:6]
    zg_send, zg_recv, xg_send, xg_recv, cg_send, cg_recv = sems[6:]

    n_rows, hidden = p_ref.shape
    half = hidden // 2
    quarter = half // nx
    width = quarter // nch
    z_rows = n_rows // nz
    group = lax.axis_index("groups")
    gene = lax.axis_index("gene")
    core = lax.axis_index("cell")
    z = gene // nx
    x = gene % nx
    other = (group, gene, 1 - core)

    def x_peer(offset):
        return (group, z * nx + (x + offset) % nx, core)

    def z_peer(offset):
        return (group, ((z + offset) % nz) * nx + x, core)

    def cols(which, block, k):
        return pl.ds(pl.multiple_of(which * half + block * quarter + k * width, 128), width)

    def part(k):
        return pl.ds(k * width, width)

    def z_block(which):
        return pl.ds(pl.multiple_of(which * z_rows, 16), z_rows)

    barrier = pltpu.get_barrier_semaphore()
    peers = [other] + [x_peer(o) for o in range(1, nx)] + [z_peer(o) for o in range(1, nz)]
    for peer in peers:
        pl.semaphore_signal(barrier, inc=1, device_id=peer, device_id_type=MESH)
    pl.semaphore_wait(barrier, len(peers))

    def remote(src, dst, send, recv, peer):
        copy = pltpu.make_async_remote_copy(
            src_ref=src,
            dst_ref=dst,
            send_sem=send,
            recv_sem=recv,
            device_id=peer,
            device_id_type=MESH,
        )
        copy.start()
        return copy

    started = {}

    def stage0(k):
        started["c", k] = [
            remote(
                p_ref.at[:, cols(1 - core, (x + o) % nx, k)],
                c_buf.at[o, :, part(k)],
                cs_send.at[k, o],
                cs_recv.at[k, o],
                other,
            )
            for o in list(range(1, nx)) + [0]
        ]

    def stage1(k):
        for copy in started["c", k]:
            copy.wait_recv()
        for o in range(1, nx):
            mine = cols(core, (x + o) % nx, k)

            def add(rows, _):
                s1_buf[o - 1, rows, part(k)] = (
                    p_ref[rows, mine].astype(F32) + c_buf[o, rows, part(k)].astype(F32)
                ).astype(BF16)

            row_loop(n_rows, 32, add)
        started["x", k] = [
            remote(
                s1_buf.at[o - 1, :, part(k)],
                x_buf.at[o - 1, :, part(k)],
                xs_send.at[k, o - 1],
                xs_recv.at[k, o - 1],
                x_peer(o),
            )
            for o in range(1, nx)
        ]

    def stage2(k):
        for copy in started["x", k]:
            copy.wait_recv()
        mine = cols(core, x, k)

        def add(rows, _):
            total = p_ref[rows, mine].astype(F32) + c_buf[0, rows, part(k)].astype(F32)
            for o in range(1, nx):
                total = total + x_buf[o - 1, rows, part(k)].astype(F32)
            s2_buf[rows, part(k)] = total.astype(BF16)

        row_loop(n_rows, 32, add)
        started["z", k] = [
            remote(
                s2_buf.at[z_block((z + o) % nz), part(k)],
                z_buf.at[o - 1, :, part(k)],
                zs_send.at[k, o - 1],
                zs_recv.at[k, o - 1],
                z_peer(o),
            )
            for o in range(1, nz)
        ]

    def stage3(k):
        for copy in started["z", k]:
            copy.wait_recv()
        mine = cols(core, x, k)

        def finish(rows, start):
            own = pl.ds(pl.multiple_of(z * z_rows + start, 16), 16)
            total = p_ref[own, mine].astype(F32) + c_buf[0, own, part(k)].astype(F32)
            for o in range(1, nx):
                total = total + x_buf[o - 1, own, part(k)].astype(F32)
            for o in range(1, nz):
                total = total + z_buf[o - 1, rows, part(k)].astype(F32)
            if kind == "enc":
                e_ref[rows, part(k)] = total
                value = total / (1.0 + jnp.exp(-total))
            elif kind == "crit":
                value = -weight_ref[own, :] * readout_ref[:, mine] * silu_grad(total)
            else:
                value = silu_grad(e_ref[rows, part(k)]) * total
            g_ref[own, mine] = value.astype(BF16)

        row_loop(z_rows, 16, finish)
        block = g_ref.at[z_block(z), mine]
        started["zg", k] = [
            remote(block, block, zg_send.at[k, o - 1], zg_recv.at[k, o - 1], z_peer(o))
            for o in range(1, nz)
        ]

    def stage4(k):
        for copy in started["zg", k]:
            copy.wait_recv()
        block = g_ref.at[:, cols(core, x, k)]
        started["xg", k] = [
            remote(block, block, xg_send.at[k, o - 1], xg_recv.at[k, o - 1], x_peer(o))
            for o in range(1, nx)
        ]
        started["cg", k] = [remote(block, block, cg_send.at[k, 0], cg_recv.at[k, 0], other)]

    def stage5(k):
        for o, copy in enumerate(started["xg", k], 1):
            copy.wait_recv()
            block = g_ref.at[:, cols(core, (x + nx - o) % nx, k)]
            started["cg", k].append(
                remote(block, block, cg_send.at[k, o], cg_recv.at[k, o], other)
            )

    def stage6(k):
        for copy in started["cg", k]:
            copy.wait_recv()

    stages = (stage0, stage1, stage2, stage3, stage4, stage5, stage6)
    for k in range(nch):
        stage0(k)
    for step in range(1, nch + len(stages) - 1):
        for index in range(len(stages) - 1, 0, -1):
            if 0 <= step - index < nch:
                stages[index](step - index)
    for copies in started.values():
        for copy in copies:
            copy.wait_send()


def exchange(kind, partial, extras, n_gene):
    nx = 2 if n_gene <= 8 else 4
    nz = n_gene // nx
    n_rows, hidden = partial.shape
    quarter = hidden // (2 * nx)
    nch = min(4, quarter // 128)
    gathered = jax.ShapeDtypeStruct((n_rows, hidden), BF16)
    vmem = pl.BlockSpec(memory_space=pltpu.VMEM)
    if kind == "enc":
        out_shape = (gathered, jax.ShapeDtypeStruct((n_rows // nz, quarter), F32))
        out_specs = (vmem, vmem)
    else:
        out_shape, out_specs = gathered, vmem
    dma = pltpu.SemaphoreType.DMA
    counts = (nx, nx, nx - 1, nx - 1, nz - 1, nz - 1, nz - 1, nz - 1, nx - 1, nx - 1, nx, nx)
    return pl.pallas_call(
        functools.partial(exchange_kernel, kind, nz, nx, nch),
        out_shape=out_shape,
        in_specs=[vmem] * (1 + len(extras)),
        out_specs=out_specs,
        scratch_shapes=[
            pltpu.VMEM((nx, n_rows, quarter), BF16),
            pltpu.VMEM((nx - 1, n_rows, quarter), BF16),
            pltpu.VMEM((nx - 1, n_rows, quarter), BF16),
            pltpu.VMEM((n_rows, quarter), BF16),
            pltpu.VMEM((nz - 1, n_rows // nz, quarter), BF16),
        ]
        + [dma((nch, count)) for count in counts],
        compiler_params=pltpu.CompilerParams(
            collective_id={"enc": 0, "crit": 1, "lat": 2}[kind],
            has_side_effects=True,
            vmem_limit_bytes=40 * 1024 * 1024,
        ),
    )(partial, *extras)


def paired_rows(perturbed, pair_index):
    per_block = pair_index.shape[1]
    one_hot = (
        pair_index.reshape(per_block)[:, None] == jnp.arange(per_block, dtype=jnp.int32)[None, :]
    ).astype(perturbed.dtype)
    return jnp.dot(one_hot, perturbed, preferred_element_type=F32).astype(perturbed.dtype)


def shards(
    control, perturbed, pair_index, noise_draws, cell_mass, w_enc, w_dec, w_crit, w_noise, readout
):
    n_gene = lax.axis_size("gene")
    n_draws = noise_draws.shape[1]
    control_all = lax.all_to_all(control, "cell", split_axis=1, concat_axis=0, tiled=True)
    n_cells, n_genes = control_all.shape
    n_pairs = n_cells * n_draws
    hidden = w_enc.shape[1]
    w_noise_all = lax.all_gather(w_noise, "gene", axis=1, tiled=True)
    readout_all = lax.all_gather(readout, "gene", axis=0, tiled=True)
    noise_all = lax.all_gather(noise_draws.transpose(1, 0, 2), "cell", axis=1, tiled=True)
    mass_all = lax.all_gather(cell_mass, "cell", axis=0, tiled=True)
    target = lax.all_to_all(
        paired_rows(perturbed, pair_index), "cell", split_axis=1, concat_axis=0, tiled=True
    )

    enc_part = contract(control_all, w_enc, 1, 0).astype(BF16)
    silu_enc, enc_own = exchange("enc", enc_part, (), n_gene)
    shift = contract(noise_all.reshape(n_pairs, noise_all.shape[2]), w_noise_all, 1, 0)
    latent = (
        (silu_enc.astype(F32)[None] + shift.reshape(n_draws, n_cells, hidden))
        .astype(BF16)
        .reshape(n_pairs, hidden)
    )
    decoded = contract(latent, w_dec, 1, 1).reshape(n_draws, n_cells, n_genes)
    moved = (control_all.astype(F32)[None] + decoded).astype(BF16)
    crit_part = contract(moved.reshape(n_pairs, n_genes), w_crit, 1, 0).astype(BF16)
    weight = jnp.tile(8.0 / n_draws * mass_all, n_draws)[:, None]
    critic_grad = exchange("crit", crit_part, (weight, readout_all[None, :]), n_gene)
    critic_back = contract(critic_grad, w_crit, 1, 1).reshape(n_draws, n_cells, n_genes)
    moved_f32 = moved.astype(F32)
    mean_moved = jnp.sum(moved_f32, axis=0) / n_draws
    cost_grad = (
        8.0
        / (n_draws * math.sqrt(G))
        * mass_all[None, :, None]
        * (0.5 * moved_f32 + (0.5 * mean_moved - target.astype(F32))[None])
    )
    moved_grad = (cost_grad + critic_back).astype(BF16)
    summed = jnp.sum(moved_grad.astype(F32), axis=0).astype(BF16)
    lat_part = contract(summed, w_dec, 1, 0).astype(BF16)
    enc_grad = exchange("lat", lat_part, (enc_own,), n_gene)
    grad_dec = contract(moved_grad.reshape(n_pairs, n_genes), latent, 0, 0).astype(BF16)
    grad_enc = contract(control_all, enc_grad, 0, 0).astype(BF16)
    return (grad_enc, grad_dec)


def solution(mesh):
    placed = (
        P(("groups", "cell"), "gene"),
        P(("groups", "cell"), "gene"),
        P(("groups", "cell"), None),
        P(("groups", "cell"), None, None),
        P(("groups", "cell")),
        P(("gene", "cell"), None),
        P(("gene", "cell"), None),
        P(("gene", "cell"), None),
        P(None, "gene"),
        P("gene"),
    )
    return jax.shard_map(
        shards,
        mesh=mesh,
        in_specs=placed,
        out_specs=(P(("groups", "gene", "cell"), None), P(("groups", "gene", "cell"), None)),
        check_vma=False,
    )
```

```python
import functools
import math

import jax
import jax.numpy as jnp
from jax import lax
from jax.experimental import pallas as pl
from jax.experimental.pallas import tpu as pltpu
from jax.sharding import PartitionSpec as P

G = 32768
MESH = pl.DeviceIdType.MESH
F32 = jnp.float32
BF16 = jnp.bfloat16


def silu_grad(inputs):
    sigmoid = 1.0 / (1.0 + jnp.exp(-inputs))
    return sigmoid * (1.0 + inputs * (1.0 - sigmoid))


def contract(former, latter, former_dim, latter_dim):
    return lax.dot_general(
        former,
        latter,
        (((former_dim,), (latter_dim,)), ((), ())),
        preferred_element_type=F32,
    )


def row_loop(n_rows, tile, body):
    def step(i, carry):
        body(pl.ds(pl.multiple_of(i * tile, tile), tile), pl.multiple_of(i * tile, tile))
        return carry

    lax.fori_loop(0, n_rows // tile, step, 0)


def exchange_kernel(kind, nz, nx, nch, *refs):
    if kind == "enc":
        p_ref, noise_ref, mass_ref, g_ref, e_ref, noise_all, mass_all = refs[:7]
        rest = refs[7:]
    elif kind == "crit":
        p_ref, weight_ref, readout_ref, g_ref = refs[:4]
        rest = refs[4:]
    else:
        p_ref, e_ref, g_ref = refs[:3]
        rest = refs[3:]
    (c_buf, s1_buf, x_buf, s2_buf, z_buf) = rest[:5]
    sems = rest[5:17]
    small_send, small_recv = rest[17:]
    cs_send, cs_recv, xs_send, xs_recv, zs_send, zs_recv = sems[:6]
    zg_send, zg_recv, xg_send, xg_recv, cg_send, cg_recv = sems[6:]

    n_rows, hidden = p_ref.shape
    half = hidden // 2
    quarter = half // nx
    width = quarter // nch
    z_rows = n_rows // nz
    group = lax.axis_index("groups")
    gene = lax.axis_index("gene")
    core = lax.axis_index("cell")
    z = gene // nx
    x = gene % nx
    other = (group, gene, 1 - core)

    def x_peer(offset):
        return (group, z * nx + (x + offset) % nx, core)

    def z_peer(offset):
        return (group, ((z + offset) % nz) * nx + x, core)

    def cols(which, block, k):
        return pl.ds(pl.multiple_of(which * half + block * quarter + k * width, 128), width)

    def part(k):
        return pl.ds(k * width, width)

    def z_block(which):
        return pl.ds(pl.multiple_of(which * z_rows, 16), z_rows)

    barrier = pltpu.get_barrier_semaphore()
    peers = [other] + [x_peer(o) for o in range(1, nx)] + [z_peer(o) for o in range(1, nz)]
    for peer in peers:
        pl.semaphore_signal(barrier, inc=1, device_id=peer, device_id_type=MESH)
    pl.semaphore_wait(barrier, len(peers))

    def remote(src, dst, send, recv, peer):
        copy = pltpu.make_async_remote_copy(
            src_ref=src,
            dst_ref=dst,
            send_sem=send,
            recv_sem=recv,
            device_id=peer,
            device_id_type=MESH,
        )
        copy.start()
        return copy

    started = {}

    def stage0(k):
        started["c", k] = [
            remote(
                p_ref.at[:, cols(1 - core, (x + o) % nx, k)],
                c_buf.at[o, :, part(k)],
                cs_send.at[k, o],
                cs_recv.at[k, o],
                other,
            )
            for o in list(range(1, nx)) + [0]
        ]

    def stage1(k):
        for copy in started["c", k]:
            copy.wait_recv()
        for o in range(1, nx):
            mine = cols(core, (x + o) % nx, k)

            def add(rows, _):
                s1_buf[o - 1, rows, part(k)] = (
                    p_ref[rows, mine].astype(F32) + c_buf[o, rows, part(k)].astype(F32)
                ).astype(BF16)

            row_loop(n_rows, 32, add)
        started["x", k] = [
            remote(
                s1_buf.at[o - 1, :, part(k)],
                x_buf.at[o - 1, :, part(k)],
                xs_send.at[k, o - 1],
                xs_recv.at[k, o - 1],
                x_peer(o),
            )
            for o in range(1, nx)
        ]

    def stage2(k):
        for copy in started["x", k]:
            copy.wait_recv()
        mine = cols(core, x, k)

        def add(rows, _):
            total = p_ref[rows, mine].astype(F32) + c_buf[0, rows, part(k)].astype(F32)
            for o in range(1, nx):
                total = total + x_buf[o - 1, rows, part(k)].astype(F32)
            s2_buf[rows, part(k)] = total.astype(BF16)

        row_loop(n_rows, 32, add)
        started["z", k] = [
            remote(
                s2_buf.at[z_block((z + o) % nz), part(k)],
                z_buf.at[o - 1, :, part(k)],
                zs_send.at[k, o - 1],
                zs_recv.at[k, o - 1],
                z_peer(o),
            )
            for o in range(1, nz)
        ]

    def stage3(k):
        for copy in started["z", k]:
            copy.wait_recv()
        mine = cols(core, x, k)

        def finish(rows, start):
            own = pl.ds(pl.multiple_of(z * z_rows + start, 16), 16)
            total = p_ref[own, mine].astype(F32) + c_buf[0, own, part(k)].astype(F32)
            for o in range(1, nx):
                total = total + x_buf[o - 1, own, part(k)].astype(F32)
            for o in range(1, nz):
                total = total + z_buf[o - 1, rows, part(k)].astype(F32)
            if kind == "enc":
                e_ref[rows, part(k)] = total
                value = total / (1.0 + jnp.exp(-total))
            elif kind == "crit":
                value = -weight_ref[own, :] * readout_ref[:, mine] * silu_grad(total)
            else:
                value = silu_grad(e_ref[rows, part(k)]) * total
            g_ref[own, mine] = value.astype(BF16)

        row_loop(z_rows, 16, finish)
        block = g_ref.at[z_block(z), mine]
        started["zg", k] = [
            remote(block, block, zg_send.at[k, o - 1], zg_recv.at[k, o - 1], z_peer(o))
            for o in range(1, nz)
        ]

    def stage4(k):
        for copy in started["zg", k]:
            copy.wait_recv()
        block = g_ref.at[:, cols(core, x, k)]
        started["xg", k] = [
            remote(block, block, xg_send.at[k, o - 1], xg_recv.at[k, o - 1], x_peer(o))
            for o in range(1, nx)
        ]
        started["cg", k] = [remote(block, block, cg_send.at[k, 0], cg_recv.at[k, 0], other)]

    def stage5(k):
        for o, copy in enumerate(started["xg", k], 1):
            copy.wait_recv()
            block = g_ref.at[:, cols(core, (x + nx - o) % nx, k)]
            started["cg", k].append(
                remote(block, block, cg_send.at[k, o], cg_recv.at[k, o], other)
            )

    def stage6(k):
        for copy in started["cg", k]:
            copy.wait_recv()

    small = []
    if kind == "enc":
        cells = noise_ref.shape[1]
        own_cells = pl.ds(pl.multiple_of(core * cells, 16), cells)
        small = [
            remote(noise_ref, noise_all.at[:, own_cells, :], small_send.at[0], small_recv.at[0], other),
            remote(mass_ref, mass_all.at[core], small_send.at[1], small_recv.at[1], other),
        ]
        noise_all[:, own_cells, :] = noise_ref[...]
        mass_all[core] = mass_ref[...]
    stages = (stage0, stage1, stage2, stage3, stage4, stage5, stage6)
    for k in range(nch):
        stage0(k)
    for step in range(1, nch + len(stages) - 1):
        for index in range(len(stages) - 1, 0, -1):
            if 0 <= step - index < nch:
                stages[index](step - index)
    for copy in small:
        copy.wait_recv()
    started["small"] = small
    for copies in started.values():
        for copy in copies:
            copy.wait_send()


def exchange(kind, partial, extras, n_gene):
    nx = 2 if n_gene <= 8 else 4
    nz = n_gene // nx
    n_rows, hidden = partial.shape
    quarter = hidden // (2 * nx)
    nch = min(4, quarter // 128)
    gathered = jax.ShapeDtypeStruct((n_rows, hidden), BF16)
    vmem = pl.BlockSpec(memory_space=pltpu.VMEM)
    if kind == "enc":
        noise, mass = extras
        out_shape = (
            gathered,
            jax.ShapeDtypeStruct((n_rows // nz, quarter), F32),
            jax.ShapeDtypeStruct((noise.shape[0], 2 * noise.shape[1], noise.shape[2]), BF16),
            jax.ShapeDtypeStruct((2,) + mass.shape, F32),
        )
        out_specs = (vmem,) * 4
    else:
        out_shape, out_specs = gathered, vmem
    dma = pltpu.SemaphoreType.DMA
    counts = (nx, nx, nx - 1, nx - 1, nz - 1, nz - 1, nz - 1, nz - 1, nx - 1, nx - 1, nx, nx)
    return pl.pallas_call(
        functools.partial(exchange_kernel, kind, nz, nx, nch),
        out_shape=out_shape,
        in_specs=[vmem] * (1 + len(extras)),
        out_specs=out_specs,
        scratch_shapes=[
            pltpu.VMEM((nx, n_rows, quarter), BF16),
            pltpu.VMEM((nx - 1, n_rows, quarter), BF16),
            pltpu.VMEM((nx - 1, n_rows, quarter), BF16),
            pltpu.VMEM((n_rows, quarter), BF16),
            pltpu.VMEM((nz - 1, n_rows // nz, quarter), BF16),
        ]
        + [dma((nch, count)) for count in counts]
        + [dma((2,)), dma((2,))],
        compiler_params=pltpu.CompilerParams(
            collective_id={"enc": 0, "crit": 1, "lat": 2}[kind],
            has_side_effects=True,
            vmem_limit_bytes=40 * 1024 * 1024,
        ),
    )(partial, *extras)


def outer_kernel(left_ref, right_ref, out_ref):
    width = min(1024, right_ref.shape[1])

    def step(i, carry):
        cols = pl.ds(pl.multiple_of(i * width, width), width)
        out_ref[:, cols] = contract(left_ref[...], right_ref[:, cols], 0, 0).astype(BF16)
        return carry

    lax.fori_loop(0, right_ref.shape[1] // width, step, 0)


def outer_sum(left, right):
    depth, n_left = left.shape
    n_right = right.shape[1]
    tile = min(256, n_left)
    return pl.pallas_call(
        outer_kernel,
        grid=(n_left // tile,),
        out_shape=jax.ShapeDtypeStruct((n_left, n_right), BF16),
        in_specs=[
            pl.BlockSpec((depth, tile), lambda i: (0, i)),
            pl.BlockSpec((depth, n_right), lambda i: (0, 0)),
        ],
        out_specs=pl.BlockSpec((tile, n_right), lambda i: (i, 0)),
        compiler_params=pltpu.CompilerParams(vmem_limit_bytes=32 * 1024 * 1024),
        cost_estimate=pl.CostEstimate(
            flops=2 * depth * n_left * n_right,
            bytes_accessed=2 * (n_left * n_right + depth * (n_left + n_right)),
            transcendentals=0,
        ),
    )(left, right)


def paired_rows(perturbed, pair_index):
    per_block = pair_index.shape[1]
    one_hot = (
        pair_index.reshape(per_block)[:, None] == jnp.arange(per_block, dtype=jnp.int32)[None, :]
    ).astype(perturbed.dtype)
    return jnp.dot(one_hot, perturbed, preferred_element_type=F32).astype(perturbed.dtype)


def shards(
    control, perturbed, pair_index, noise_draws, cell_mass, w_enc, w_dec, w_crit, w_noise, readout
):
    n_gene = lax.axis_size("gene")
    n_draws = noise_draws.shape[1]
    control_all = lax.all_to_all(control, "cell", split_axis=1, concat_axis=0, tiled=True)
    n_cells, n_genes = control_all.shape
    n_pairs = n_cells * n_draws
    hidden = w_enc.shape[1]
    n_noise = w_noise.shape[0]
    high = lax.reduce_precision(readout, 8, 7)
    middle = lax.reduce_precision(readout - high, 8, 7)
    terms = jnp.stack([high, middle, readout - high - middle]).astype(BF16)
    terms = jnp.pad(terms, ((0, 13), (0, 0)))
    packed = lax.all_gather(
        jnp.concatenate([w_noise, terms], axis=0), "gene", axis=1, tiled=True
    )
    w_noise_all = packed[:n_noise]
    target = lax.all_to_all(
        paired_rows(perturbed, pair_index), "cell", split_axis=1, concat_axis=0, tiled=True
    )

    enc_part = contract(control_all, w_enc, 1, 0).astype(BF16)
    mass_rows = jnp.broadcast_to(cell_mass[None, :], (8, cell_mass.shape[0]))
    silu_enc, enc_own, noise_all, mass_all = exchange(
        "enc", enc_part, (noise_draws.transpose(1, 0, 2), mass_rows), n_gene
    )
    mass_all = mass_all[:, 0, :].reshape(n_cells)
    read = packed[n_noise : n_noise + 3].astype(F32)
    readout_all = read[0] + (read[1] + read[2])
    shift = contract(noise_all.reshape(n_pairs, noise_all.shape[2]), w_noise_all, 1, 0)
    latent = (
        (silu_enc.astype(F32)[None] + shift.reshape(n_draws, n_cells, hidden))
        .astype(BF16)
        .reshape(n_pairs, hidden)
    )
    decoded = contract(latent, w_dec, 1, 1).reshape(n_draws, n_cells, n_genes)
    moved = (control_all.astype(F32)[None] + decoded).astype(BF16)
    crit_part = contract(moved.reshape(n_pairs, n_genes), w_crit, 1, 0).astype(BF16)
    weight = jnp.tile(8.0 / n_draws * mass_all, n_draws)[:, None]
    critic_grad = exchange("crit", crit_part, (weight, readout_all[None, :]), n_gene)
    critic_back = contract(critic_grad, w_crit, 1, 1).reshape(n_draws, n_cells, n_genes)
    moved_f32 = moved.astype(F32)
    mean_moved = jnp.sum(moved_f32, axis=0) / n_draws
    cost_grad = (
        8.0
        / (n_draws * math.sqrt(G))
        * mass_all[None, :, None]
        * (0.5 * moved_f32 + (0.5 * mean_moved - target.astype(F32))[None])
    )
    moved_grad = (cost_grad + critic_back).astype(BF16)
    summed = jnp.sum(moved_grad.astype(F32), axis=0).astype(BF16)
    lat_part = contract(summed, w_dec, 1, 0).astype(BF16)
    enc_grad = exchange("lat", lat_part, (enc_own,), n_gene)
    grad_dec = contract(moved_grad.reshape(n_pairs, n_genes), latent, 0, 0).astype(BF16)
    grad_enc = outer_sum(control_all, enc_grad)
    return (grad_enc, grad_dec)


def solution(mesh):
    placed = (
        P(("groups", "cell"), "gene"),
        P(("groups", "cell"), "gene"),
        P(("groups", "cell"), None),
        P(("groups", "cell"), None, None),
        P(("groups", "cell")),
        P(("gene", "cell"), None),
        P(("gene", "cell"), None),
        P(("gene", "cell"), None),
        P(None, "gene"),
        P("gene"),
    )
    return jax.shard_map(
        shards,
        mesh=mesh,
        in_specs=placed,
        out_specs=(P(("groups", "gene", "cell"), None), P(("groups", "gene", "cell"), None)),
        check_vma=False,
    )
```

```python
import functools
import math

import jax
import jax.numpy as jnp
from jax import lax
from jax.experimental import pallas as pl
from jax.experimental.pallas import tpu as pltpu
from jax.sharding import PartitionSpec as P

G = 32768
MESH = pl.DeviceIdType.MESH
F32 = jnp.float32
BF16 = jnp.bfloat16


def silu_grad(inputs):
    sigmoid = 1.0 / (1.0 + jnp.exp(-inputs))
    return sigmoid * (1.0 + inputs * (1.0 - sigmoid))


def contract(former, latter, former_dim, latter_dim):
    return lax.dot_general(
        former,
        latter,
        (((former_dim,), (latter_dim,)), ((), ())),
        preferred_element_type=F32,
    )


def row_loop(n_rows, tile, body):
    def step(i, carry):
        body(pl.ds(pl.multiple_of(i * tile, tile), tile), pl.multiple_of(i * tile, tile))
        return carry

    lax.fori_loop(0, n_rows // tile, step, 0)


def exchange_kernel(kind, nz, nx, nch, *refs):
    a_ref, w_ref = refs[:2]
    refs = refs[2:]
    if kind == "enc":
        noise_ref, mass_ref, g_ref, e_ref, noise_all, mass_all = refs[:6]
        rest = refs[6:]
    elif kind == "crit":
        weight_ref, readout_ref, g_ref = refs[:3]
        rest = refs[3:]
    else:
        e_ref, g_ref = refs[:2]
        rest = refs[2:]
    (c_buf, s1_buf, x_buf, s2_buf, z_buf) = rest[:5]
    sems = rest[5:17]
    small_send, small_recv, p_ref, w_buf, w_sem = rest[17:]
    cs_send, cs_recv, xs_send, xs_recv, zs_send, zs_recv = sems[:6]
    zg_send, zg_recv, xg_send, xg_recv, cg_send, cg_recv = sems[6:]

    n_rows, hidden = g_ref.shape
    half = hidden // 2
    quarter = half // nx
    width = quarter // nch
    z_rows = n_rows // nz
    group = lax.axis_index("groups")
    gene = lax.axis_index("gene")
    core = lax.axis_index("cell")
    z = gene // nx
    x = gene % nx
    other = (group, gene, 1 - core)

    def x_peer(offset):
        return (group, z * nx + (x + offset) % nx, core)

    def z_peer(offset):
        return (group, ((z + offset) % nz) * nx + x, core)

    def cols(which, block, k):
        return pl.ds(pl.multiple_of(which * half + block * quarter + k * width, 128), width)

    def part(k):
        return pl.ds(k * width, width)

    def z_block(which):
        return pl.ds(pl.multiple_of(which * z_rows, 16), z_rows)

    order = list(range(1, nx)) + [0]
    tiles = [(own, o, k) for k in range(nch) for own in (0, 1) for o in order]
    slots = w_buf.shape[0]

    def tile_cols(own, o, k):
        return cols(core if own else 1 - core, (x + o) % nx, k)

    def fetch(n):
        copy = pltpu.make_async_copy(
            w_ref.at[:, tile_cols(*tiles[n])], w_buf.at[n % slots], w_sem.at[n % slots]
        )
        copy.start()
        return copy

    fetched = [fetch(n) for n in range(slots)]

    def multiply(*tile):
        n = tiles.index(tile)
        fetched[n].wait()
        where = tile_cols(*tile)

        def dot(rows, _):
            p_ref[rows, where] = contract(a_ref[rows, :], w_buf[n % slots], 1, 0).astype(BF16)

        row_loop(n_rows, min(256, n_rows), dot)
        if n + slots < len(tiles):
            fetched.append(fetch(n + slots))

    barrier = pltpu.get_barrier_semaphore()
    peers = [other] + [x_peer(o) for o in range(1, nx)] + [z_peer(o) for o in range(1, nz)]
    for peer in peers:
        pl.semaphore_signal(barrier, inc=1, device_id=peer, device_id_type=MESH)
    pl.semaphore_wait(barrier, len(peers))

    def remote(src, dst, send, recv, peer):
        copy = pltpu.make_async_remote_copy(
            src_ref=src,
            dst_ref=dst,
            send_sem=send,
            recv_sem=recv,
            device_id=peer,
            device_id_type=MESH,
        )
        copy.start()
        return copy

    started = {}

    def stage0(k):
        started["c", k] = []
        for o in order:
            multiply(0, o, k)
            started["c", k].append(
                remote(
                    p_ref.at[:, tile_cols(0, o, k)],
                    c_buf.at[o, :, part(k)],
                    cs_send.at[k, o],
                    cs_recv.at[k, o],
                    other,
                )
            )
        for o in order:
            multiply(1, o, k)

    def stage1(k):
        for copy in started["c", k]:
            copy.wait_recv()
        for o in range(1, nx):
            mine = cols(core, (x + o) % nx, k)

            def add(rows, _):
                s1_buf[o - 1, rows, part(k)] = (
                    p_ref[rows, mine].astype(F32) + c_buf[o, rows, part(k)].astype(F32)
                ).astype(BF16)

            row_loop(n_rows, 32, add)
        started["x", k] = [
            remote(
                s1_buf.at[o - 1, :, part(k)],
                x_buf.at[o - 1, :, part(k)],
                xs_send.at[k, o - 1],
                xs_recv.at[k, o - 1],
                x_peer(o),
            )
            for o in range(1, nx)
        ]

    def stage2(k):
        for copy in started["x", k]:
            copy.wait_recv()
        mine = cols(core, x, k)

        def add(rows, _):
            total = p_ref[rows, mine].astype(F32) + c_buf[0, rows, part(k)].astype(F32)
            for o in range(1, nx):
                total = total + x_buf[o - 1, rows, part(k)].astype(F32)
            s2_buf[rows, part(k)] = total.astype(BF16)

        row_loop(n_rows, 32, add)
        started["z", k] = [
            remote(
                s2_buf.at[z_block((z + o) % nz), part(k)],
                z_buf.at[o - 1, :, part(k)],
                zs_send.at[k, o - 1],
                zs_recv.at[k, o - 1],
                z_peer(o),
            )
            for o in range(1, nz)
        ]

    def stage3(k):
        for copy in started["z", k]:
            copy.wait_recv()
        mine = cols(core, x, k)

        def finish(rows, start):
            own = pl.ds(pl.multiple_of(z * z_rows + start, 16), 16)
            total = p_ref[own, mine].astype(F32) + c_buf[0, own, part(k)].astype(F32)
            for o in range(1, nx):
                total = total + x_buf[o - 1, own, part(k)].astype(F32)
            for o in range(1, nz):
                total = total + z_buf[o - 1, rows, part(k)].astype(F32)
            if kind == "enc":
                e_ref[rows, part(k)] = total
                value = total / (1.0 + jnp.exp(-total))
            elif kind == "crit":
                value = -weight_ref[own, :] * readout_ref[:, mine] * silu_grad(total)
            else:
                value = silu_grad(e_ref[rows, part(k)]) * total
            g_ref[own, mine] = value.astype(BF16)

        row_loop(z_rows, 16, finish)
        block = g_ref.at[z_block(z), mine]
        started["zg", k] = [
            remote(block, block, zg_send.at[k, o - 1], zg_recv.at[k, o - 1], z_peer(o))
            for o in range(1, nz)
        ]

    def stage4(k):
        for copy in started["zg", k]:
            copy.wait_recv()
        block = g_ref.at[:, cols(core, x, k)]
        started["xg", k] = [
            remote(block, block, xg_send.at[k, o - 1], xg_recv.at[k, o - 1], x_peer(o))
            for o in range(1, nx)
        ]
        started["cg", k] = [remote(block, block, cg_send.at[k, 0], cg_recv.at[k, 0], other)]

    def stage5(k):
        for o, copy in enumerate(started["xg", k], 1):
            copy.wait_recv()
            block = g_ref.at[:, cols(core, (x + nx - o) % nx, k)]
            started["cg", k].append(
                remote(block, block, cg_send.at[k, o], cg_recv.at[k, o], other)
            )

    def stage6(k):
        for copy in started["cg", k]:
            copy.wait_recv()

    small = []
    if kind == "enc":
        cells = noise_ref.shape[1]
        own_cells = pl.ds(pl.multiple_of(core * cells, 16), cells)
        small = [
            remote(noise_ref, noise_all.at[:, own_cells, :], small_send.at[0], small_recv.at[0], other),
            remote(mass_ref, mass_all.at[core], small_send.at[1], small_recv.at[1], other),
        ]
        noise_all[:, own_cells, :] = noise_ref[...]
        mass_all[core] = mass_ref[...]
    stages = (stage0, stage1, stage2, stage3, stage4, stage5, stage6)
    for step in range(nch + len(stages) - 1):
        if step < nch:
            stage0(step)
        for index in range(len(stages) - 1, 0, -1):
            if 0 <= step - index < nch:
                stages[index](step - index)
    for copy in small:
        copy.wait_recv()
    started["small"] = small
    for copies in started.values():
        for copy in copies:
            copy.wait_send()


def exchange(kind, former, weight, extras, n_gene):
    nx = 2 if n_gene <= 8 else 4
    nz = n_gene // nx
    n_rows, depth = former.shape
    hidden = weight.shape[1]
    quarter = hidden // (2 * nx)
    nch = min(4, quarter // 128)
    gathered = jax.ShapeDtypeStruct((n_rows, hidden), BF16)
    vmem = pl.BlockSpec(memory_space=pltpu.VMEM)
    if kind == "enc":
        noise, mass = extras
        out_shape = (
            gathered,
            jax.ShapeDtypeStruct((n_rows // nz, quarter), F32),
            jax.ShapeDtypeStruct((noise.shape[0], 2 * noise.shape[1], noise.shape[2]), BF16),
            jax.ShapeDtypeStruct((2,) + mass.shape, F32),
        )
        out_specs = (vmem,) * 4
    else:
        out_shape, out_specs = gathered, vmem
    dma = pltpu.SemaphoreType.DMA
    counts = (nx, nx, nx - 1, nx - 1, nz - 1, nz - 1, nz - 1, nz - 1, nx - 1, nx - 1, nx, nx)
    return pl.pallas_call(
        functools.partial(exchange_kernel, kind, nz, nx, nch),
        out_shape=out_shape,
        in_specs=[vmem, pl.BlockSpec(memory_space=pl.ANY)] + [vmem] * len(extras),
        out_specs=out_specs,
        scratch_shapes=[
            pltpu.VMEM((nx, n_rows, quarter), BF16),
            pltpu.VMEM((nx - 1, n_rows, quarter), BF16),
            pltpu.VMEM((nx - 1, n_rows, quarter), BF16),
            pltpu.VMEM((n_rows, quarter), BF16),
            pltpu.VMEM((nz - 1, n_rows // nz, quarter), BF16),
        ]
        + [dma((nch, count)) for count in counts]
        + [dma((2,)), dma((2,))]
        + [
            pltpu.VMEM((n_rows, hidden), BF16),
            pltpu.VMEM((3, depth, quarter // nch), BF16),
            dma((3,)),
        ],
        compiler_params=pltpu.CompilerParams(
            collective_id={"enc": 0, "crit": 1, "lat": 2}[kind],
            has_side_effects=True,
            vmem_limit_bytes=50 * 1024 * 1024,
        ),
    )(former, weight, *extras)


def outer_kernel(left_ref, right_ref, out_ref):
    width = min(1024, right_ref.shape[1])

    def step(i, carry):
        cols = pl.ds(pl.multiple_of(i * width, width), width)
        out_ref[:, cols] = contract(left_ref[...], right_ref[:, cols], 0, 0).astype(BF16)
        return carry

    lax.fori_loop(0, right_ref.shape[1] // width, step, 0)


def outer_sum(left, right):
    depth, n_left = left.shape
    n_right = right.shape[1]
    tile = min(256, n_left)
    return pl.pallas_call(
        outer_kernel,
        grid=(n_left // tile,),
        out_shape=jax.ShapeDtypeStruct((n_left, n_right), BF16),
        in_specs=[
            pl.BlockSpec((depth, tile), lambda i: (0, i)),
            pl.BlockSpec((depth, n_right), lambda i: (0, 0)),
        ],
        out_specs=pl.BlockSpec((tile, n_right), lambda i: (i, 0)),
        compiler_params=pltpu.CompilerParams(vmem_limit_bytes=32 * 1024 * 1024),
        cost_estimate=pl.CostEstimate(
            flops=2 * depth * n_left * n_right,
            bytes_accessed=2 * (n_left * n_right + depth * (n_left + n_right)),
            transcendentals=0,
        ),
    )(left, right)


def paired_rows(perturbed, pair_index):
    per_block = pair_index.shape[1]
    one_hot = (
        pair_index.reshape(per_block)[:, None] == jnp.arange(per_block, dtype=jnp.int32)[None, :]
    ).astype(perturbed.dtype)
    return jnp.dot(one_hot, perturbed, preferred_element_type=F32).astype(perturbed.dtype)


def shards(
    control, perturbed, pair_index, noise_draws, cell_mass, w_enc, w_dec, w_crit, w_noise, readout
):
    n_gene = lax.axis_size("gene")
    n_draws = noise_draws.shape[1]
    control_all = lax.all_to_all(control, "cell", split_axis=1, concat_axis=0, tiled=True)
    n_cells, n_genes = control_all.shape
    n_pairs = n_cells * n_draws
    hidden = w_enc.shape[1]
    n_noise = w_noise.shape[0]
    high = lax.reduce_precision(readout, 8, 7)
    middle = lax.reduce_precision(readout - high, 8, 7)
    terms = jnp.stack([high, middle, readout - high - middle]).astype(BF16)
    terms = jnp.pad(terms, ((0, 13), (0, 0)))
    packed = lax.all_gather(
        jnp.concatenate([w_noise, terms], axis=0), "gene", axis=1, tiled=True
    )
    w_noise_all = packed[:n_noise]
    target = lax.all_to_all(
        paired_rows(perturbed, pair_index), "cell", split_axis=1, concat_axis=0, tiled=True
    )

    mass_rows = jnp.broadcast_to(cell_mass[None, :], (8, cell_mass.shape[0]))
    silu_enc, enc_own, noise_all, mass_all = exchange(
        "enc", control_all, w_enc, (noise_draws.transpose(1, 0, 2), mass_rows), n_gene
    )
    mass_all = mass_all[:, 0, :].reshape(n_cells)
    read = packed[n_noise : n_noise + 3].astype(F32)
    readout_all = read[0] + (read[1] + read[2])
    shift = contract(noise_all.reshape(n_pairs, noise_all.shape[2]), w_noise_all, 1, 0)
    latent = (
        (silu_enc.astype(F32)[None] + shift.reshape(n_draws, n_cells, hidden))
        .astype(BF16)
        .reshape(n_pairs, hidden)
    )
    decoded = contract(latent, w_dec, 1, 1).reshape(n_draws, n_cells, n_genes)
    moved = (control_all.astype(F32)[None] + decoded).astype(BF16)
    weight = jnp.tile(8.0 / n_draws * mass_all, n_draws)[:, None]
    critic_grad = exchange(
        "crit",
        moved.reshape(n_pairs, n_genes),
        w_crit,
        (weight, readout_all[None, :]),
        n_gene,
    )
    critic_back = contract(critic_grad, w_crit, 1, 1).reshape(n_draws, n_cells, n_genes)
    moved_f32 = moved.astype(F32)
    mean_moved = jnp.sum(moved_f32, axis=0) / n_draws
    cost_grad = (
        8.0
        / (n_draws * math.sqrt(G))
        * mass_all[None, :, None]
        * (0.5 * moved_f32 + (0.5 * mean_moved - target.astype(F32))[None])
    )
    moved_grad = (cost_grad + critic_back).astype(BF16)
    summed = jnp.sum(moved_grad.astype(F32), axis=0).astype(BF16)
    enc_grad = exchange("lat", summed, w_dec, (enc_own,), n_gene)
    grad_dec = contract(moved_grad.reshape(n_pairs, n_genes), latent, 0, 0).astype(BF16)
    grad_enc = outer_sum(control_all, enc_grad)
    return (grad_enc, grad_dec)


def solution(mesh):
    placed = (
        P(("groups", "cell"), "gene"),
        P(("groups", "cell"), "gene"),
        P(("groups", "cell"), None),
        P(("groups", "cell"), None, None),
        P(("groups", "cell")),
        P(("gene", "cell"), None),
        P(("gene", "cell"), None),
        P(("gene", "cell"), None),
        P(None, "gene"),
        P("gene"),
    )
    return jax.shard_map(
        shards,
        mesh=mesh,
        in_specs=placed,
        out_specs=(P(("groups", "gene", "cell"), None), P(("groups", "gene", "cell"), None)),
        check_vma=False,
    )
```
